32 devices in a mesh: col: 8 (over z, x), layer: 4 (over y, core).
Axes of the slice: x: 2, y: 2, z: 4, core: 2. Of those that a mesh axis runs over, the one named last changes fastest.
Arguments:
- tangents: bfloat16 [4, 128, 128, 512], P('layer', 'col'), may hold values from -120 to 120
- voltage: float32 [2, 4, 128, 128], P(None, 'layer', 'col'), may hold values from -0.2 to 0.6
- conductance: float32 [2, 4, 128, 128], P(None, 'layer', 'col'), may hold values from 0.5 to 5
- local_weights: bfloat16 [4, 128, 7, 128, 128], P('layer', 'col'), may hold values from 0 to 0.29882812
- block_label: int32 [4, 128], replicated, may hold values 0 or 1
- pair_dest: int32 [4, 8, 32, 1], P('layer', 'col'), may hold values from 0 to 7; in each aligned block of 32 rows (0 to 31, 32 to 63, ..., all dimensions but the last counted through in order) at most 8 rows name the same one
- pair_target: int32 [4, 8, 32], P('layer', 'col'), may hold values from 0 to 15
- bundle_source: int32 [4, 8, 8], P('layer', 'col'), may hold values from 0 to 15
- pair_weights: bfloat16 [4, 8, 32, 128, 128], P('layer', 'col'), may hold values from 0 to 0.29882812
Outputs:
- next_tangents: bfloat16 [4, 128, 128, 512], P('layer', 'col')
- growth: float32 [512], replicated
The draws below stay inside these ranges and needn't reach their ends.
Inputs may be any that keep to these rules, and one draw needn't show every extreme that they name: `pair_dest`: within each group's 32 pairs no destination group is named more than 8 times, a bound that some block reaches.
All inputs are finite; a program needn't handle non-finite values.
Results may differ from the reference program's by a relative error of at most 0.019.
Values may be sent and summed in bfloat16 or wider, within the bound.
A program may use at most 192 MiB of HBM per device.

```python
import math
import jax
import jax.numpy as jnp
import numpy as np
from jax import lax

K = 512
BS = 128
LB_DEV = 1
CB_DEV = 16
P_DEV = 32
STEPS = 2
CAP = 8
NLB = 4
NCB = 128
LGROUPS = 4
CGROUPS = 8
NEURONS = 65536


def draw_tangents(key, part):
    key = jax.random.fold_in(key, 11)
    key_base, key_rows, key_cols = jax.random.split(key, 3)
    shape = (NLB, NCB, BS, K)
    row_scale = jnp.exp(jax.random.uniform(key_rows, (NLB, NCB, BS, 1), jnp.float32, 0.0, math.log(10.0)))
    col_scale = jnp.exp(jax.random.uniform(key_cols, (K,), jnp.float32, 0.0, math.log(10.0)))
    rising = jnp.exp(math.log(3.0) * jnp.arange(NCB, dtype=jnp.float32) / float(max(NCB - 1, 1)))[None, :, None, None]
    base = jax.random.truncated_normal(key_base, -4.0, 4.0, shape, jnp.float32)
    return (0.1 * base * row_scale * col_scale * rising).astype(jnp.bfloat16)


def place_ends(values, stream_key, smallest, top_value):
    index_at = [jax.random.randint(jax.random.fold_in(stream_key, axis), (), 0, length) for axis, length in enumerate(values.shape)]
    widest = values.shape.index(max(values.shape))
    beside = index_at[:widest] + [(index_at[widest] + 1) % values.shape[widest]] + index_at[widest + 1:]
    return values.at[tuple(index_at)].set(smallest).at[tuple(beside)].set(top_value)


def steps_of(rng, shape, cuts, least, top_value):
    gain, own = 1.0, jax.random.fold_in(rng, 6)
    for dim, parts in cuts:
        draws = jnp.exp(jax.random.uniform(jax.random.fold_in(own, dim), (parts,), jnp.float32, least / len(cuts), top_value / len(cuts)))
        gain = gain * jnp.repeat(draws, shape[dim] // parts).reshape([-1 if axis == dim else 1 for axis in range(len(shape))])
    return gain


def routed_block(own_key, own, number, rows, number_of, top, limit, skew):
    sequence = jax.random.permutation(own_key, number_of)
    packed, ordinary = portions_of(number_of, rows * top, limit, skew, True), portions_of(number_of, rows * top, limit, skew, False)
    places = jnp.arange(number_of)

    def named(lengths, turn):
        used = int((lengths > 0).sum())
        fixed = max(1, used // 4)
        moved = fixed + (places - fixed + turn * (used - fixed)) % max(1, number_of - fixed)
        return jnp.zeros((number_of,), jnp.int32).at[sequence[jnp.where(places < fixed, places, moved)]].set(jnp.asarray(lengths, jnp.int32))

    lengths = jnp.where(number % 4 == 0, named(packed, number // 4), named(ordinary, number - number // 4 - 1))
    mixed = jax.random.permutation(jax.random.fold_in(own, 3), number_of)
    giver, taker = mixed[0:number_of // 2 * 2:2], mixed[1:number_of // 2 * 2:2]
    margin = jnp.minimum(lengths[giver] - 1, limit - lengths[taker]) // 2
    margin = jnp.where((giver == sequence[0]) | (taker == sequence[0]) | (lengths[taker] == 0), 0, jnp.maximum(margin, 0))
    moved = jax.random.randint(jax.random.fold_in(own, 4), (number_of // 2,), 0, 1 << 20) % (margin + 1)
    lengths = lengths.at[giver].add(-moved).at[taker].add(moved)
    items = jnp.searchsorted(jnp.cumsum(lengths), jnp.arange(rows * top), side="right").astype(jnp.int32)
    table = items.reshape(top, rows).T
    table = table[jax.random.permutation(jax.random.fold_in(own, 1), rows)]
    turn = jax.random.randint(jax.random.fold_in(own, 2), (rows, 1), 0, top)
    return jnp.take_along_axis(table, (jnp.arange(top)[None, :] + turn) % top, axis=1)


def portions_of(amount, total, bound, slope, full):
    weights = [(1 << 20) // math.isqrt(standing ** slope) + 1 for standing in range(1, amount + 1)]
    largest = bound if full else min(bound, max(-(-total // amount), total * weights[0] // sum(weights)))
    least = 1 if total - largest >= amount - 1 else 0
    given, rest = [largest] + [least] * (amount - 1), total - largest - least * (amount - 1)
    while rest > 0:
        movable = [i for i in range(1, amount) if given[i] < largest] or [i for i in range(1, amount) if given[i] < bound]
        mass, remaining = sum([weights[i] for i in movable]), rest
        for i in movable:
            addition = min(bound - given[i], max(1, remaining * weights[i] // mass), rest)
            given[i] = given[i] + addition
            rest = rest - addition
    return np.array(given)


def setup_inputs(seed: int = 0) -> dict:
    key_of = jax.random.split(jax.random.key(seed), 10)
    tangents = draw_tangents(jax.random.fold_in(key_of[9], 71), 0)
    voltage = jnp.clip(-0.2 + 0.8 * jax.random.uniform(key_of[1], (STEPS, NLB, NCB, BS), jnp.float32) ** steps_of(key_of[1], (STEPS, NLB, NCB, BS), ((1, 4), (2, 8)), -0.2, 0.2), -0.2, 0.6)
    conductance = jnp.clip(jnp.exp(math.log(5.0) - 2.3025851 * jax.random.uniform(key_of[2], (STEPS, NLB, NCB, BS), jnp.float32) ** steps_of(key_of[2], (STEPS, NLB, NCB, BS), ((1, 4), (2, 8)), -0.2, 0.2)), 0.5, 5.0)
    local_weights = jnp.clip(0.29882812 * jax.random.uniform(key_of[3], (NLB, NCB, 7, BS, BS), jnp.float32) ** steps_of(key_of[3], (NLB, NCB, 7, BS, BS), ((0, 4), (1, 8)), -0.2, 0.2), 0.0, 0.29882812).astype(jnp.bfloat16)
    block_label = place_ends((jax.random.randint(key_of[4], (NLB, NCB), 0, 5) < 1).astype(jnp.int32), jax.random.fold_in(key_of[4], 1), 0, 1)
    pair_dest_keys = jax.random.split(jax.random.fold_in(key_of[5], 1), LGROUPS * CGROUPS * P_DEV // P_DEV)
    pair_dest_turns = jax.random.permutation(jax.random.fold_in(key_of[5], 3), LGROUPS * CGROUPS * P_DEV // P_DEV)
    pair_dest = jax.vmap(lambda own, number: routed_block(jax.random.fold_in(key_of[5], 2), own, number, P_DEV, CGROUPS, 1, CAP, 2))(pair_dest_keys, pair_dest_turns).reshape((LGROUPS, CGROUPS, P_DEV, 1))
    pair_target = place_ends(jax.random.randint(key_of[6], (LGROUPS, CGROUPS, P_DEV), 0, LB_DEV * CB_DEV), jax.random.fold_in(key_of[6], 1), 0, (LB_DEV * CB_DEV) - 1).astype(jnp.int32)
    bundle_source = place_ends(jax.random.randint(key_of[7], (LGROUPS, CGROUPS, CGROUPS), 0, LB_DEV * CB_DEV), jax.random.fold_in(key_of[7], 1), 0, (LB_DEV * CB_DEV) - 1).astype(jnp.int32)
    pair_weights = jnp.clip(0.29882812 * jax.random.uniform(key_of[8], (LGROUPS, CGROUPS, P_DEV, BS, BS), jnp.float32) ** steps_of(key_of[8], (LGROUPS, CGROUPS, P_DEV, BS, BS), ((0, 4), (1, 8)), -0.2, 0.2), 0.0, 0.29882812).astype(jnp.bfloat16)
    return {"tangents": tangents, "voltage": voltage, "conductance": conductance, "local_weights": local_weights, "block_label": block_label, "pair_dest": pair_dest, "pair_target": pair_target, "bundle_source": bundle_source, "pair_weights": pair_weights}


EXCITE_REVERSAL = 1.0
INHIBIT_REVERSAL = -0.5
THRESHOLD = 0.2
SIGMOID_WIDTH = 0.1
TIME_STEP = 0.1

def gain_slope(volt_now):
    sigma_value = jax.nn.sigmoid((volt_now - THRESHOLD) / SIGMOID_WIDTH)
    return sigma_value * (1.0 - sigma_value) / SIGMOID_WIDTH

def normalize(advanced, growth):
    flat_rows = advanced.reshape(-1, K)
    gram_sum = lax.dot_general(flat_rows.astype(jnp.float32), flat_rows.astype(jnp.float32), (((0,), (0,)), ((), ())), preferred_element_type=jnp.float32)
    gram_mean = gram_sum / float(NEURONS)
    lower_factor = jnp.linalg.cholesky(gram_mean)
    identity = jnp.eye(K, dtype=jnp.float32)
    lower_inverse = lax.linalg.triangular_solve(lower_factor, identity, left_side=True, lower=True)
    upper_inverse = lower_inverse.T.astype(jnp.bfloat16)
    growth = growth + jnp.log(jnp.diagonal(lower_factor))
    result = jnp.dot(flat_rows.astype(jnp.float32), upper_inverse.astype(jnp.float32), preferred_element_type=jnp.float32).astype(jnp.bfloat16)
    return (result.reshape(advanced.shape), growth)

def reference(tangents, voltage, conductance, local_weights, block_label, pair_dest, pair_target, bundle_source, pair_weights):
    reversal = jnp.where(block_label == 1, INHIBIT_REVERSAL, EXCITE_REVERSAL).astype(jnp.float32)
    destination = pair_dest[..., 0].astype(jnp.int32)
    group_layer = jnp.arange(LGROUPS, dtype=jnp.int32)[:, None, None]
    group_column = jnp.arange(CGROUPS, dtype=jnp.int32)[None, :, None]
    source_block = jnp.take_along_axis(bundle_source, destination, axis=2).astype(jnp.int32)
    zero_pairs = jnp.zeros_like(destination)
    source_layer = (group_layer * LB_DEV + source_block // CB_DEV + zero_pairs).reshape(-1).astype(jnp.int32)
    source_column = (group_column * CB_DEV + source_block % CB_DEV + zero_pairs).reshape(-1).astype(jnp.int32)
    target_layer = (group_layer * LB_DEV + pair_target // CB_DEV + zero_pairs).reshape(-1).astype(jnp.int32)
    target_column = (destination * CB_DEV + pair_target % CB_DEV).reshape(-1).astype(jnp.int32)
    flat_weights = pair_weights.reshape(-1, BS, BS)
    growth = jnp.zeros((K,), jnp.float32)
    zero_row = jnp.zeros((1, NCB, BS, K), jnp.bfloat16)
    edge_row = jnp.full((1, NCB), EXCITE_REVERSAL, jnp.float32)
    reversal_tall = jnp.concatenate([edge_row, reversal, edge_row], axis=0)
    for step_index in range(STEPS):
        volt_now = voltage[step_index]
        conduct_now = conductance[step_index]

        def scale_row(item):
            return (item[0] * gain_slope(item[1])[..., None]).astype(jnp.bfloat16)
        scaled = lax.map(scale_row, (tangents, volt_now))

        def pair_product(item):
            weight_block, layer_pos, column_pos = item
            return jnp.dot(weight_block.astype(jnp.float32), scaled[layer_pos, column_pos].astype(jnp.float32), preferred_element_type=jnp.float32).astype(jnp.bfloat16)
        products = lax.map(pair_product, (flat_weights, source_layer, source_column))
        distant = jnp.zeros((NLB, NCB, BS, K), jnp.float32).at[target_layer, target_column].add(products.astype(jnp.float32))
        padded = jnp.concatenate([zero_row, scaled, zero_row], axis=0)

        def row_update(item):
            row_index, weights_row, volt_row, conduct_row, tangent_row, distant_row = item
            middle = padded[row_index + 1]
            neighbour_rows = []
            for offset in range(5):
                neighbour_rows.append((jnp.roll(middle, 2 - offset, axis=0), jnp.roll(reversal_tall[row_index + 1], 2 - offset, axis=0)))
            neighbour_rows.append((padded[row_index], reversal_tall[row_index]))
            neighbour_rows.append((padded[row_index + 2], reversal_tall[row_index + 2]))
            drive_sum = jnp.zeros((NCB, BS, K), jnp.float32)
            for offset in range(7):
                source_rows, potential = neighbour_rows[offset]
                product_term = jnp.einsum('cij,cjk->cik', weights_row[:, offset].astype(jnp.float32), source_rows.astype(jnp.float32), precision=lax.Precision.HIGHEST)
                drive_sum = drive_sum + (potential[:, None, None] - volt_row[:, :, None]) * product_term
            drive_sum = drive_sum + (EXCITE_REVERSAL - volt_row[:, :, None]) * distant_row
            tangent_full = tangent_row.astype(jnp.float32)
            return (tangent_full + TIME_STEP * (drive_sum - conduct_row[:, :, None] * tangent_full)).astype(jnp.bfloat16)
        advanced = lax.map(row_update, (jnp.arange(NLB, dtype=jnp.int32), local_weights, volt_now, conduct_now, tangents, distant))
        tangents, growth = normalize(advanced, growth)
    return (tangents, growth)
```

```python
import functools

import jax
import jax.numpy as jnp
from jax import lax
from jax.experimental import pallas as pl
from jax.experimental.pallas import tpu as pltpu
from jax.sharding import PartitionSpec as P

EXCITE_REVERSAL = 1.0
INHIBIT_REVERSAL = -0.5
THRESHOLD = 0.2
SIGMOID_WIDTH = 0.1
TIME_STEP = 0.1
HI = lax.Precision.HIGHEST
NB = 128
ROWS = 8


def inverse_factor(block):
    n = block.shape[0]
    lane = lax.broadcasted_iota(jnp.int32, (ROWS, n), 1)
    sub = lax.broadcasted_iota(jnp.int32, (ROWS, n), 0)
    tiles = [block[t * ROWS : (t + 1) * ROWS] for t in range(n // ROWS)]
    for first in range(n // ROWS):
        start = first * ROWS
        inside = (lane >= start) & (lane < start + ROWS)
        head = tiles[first]
        cols = [jnp.broadcast_to(head[:, start + q : start + q + 1], (ROWS, n)) for q in range(ROWS)]
        head = jnp.where(lane == sub + start, 1.0, jnp.where(inside, 0.0, head))
        pivots, crossed, kept = [], [], []
        scale = jnp.zeros((ROWS, n), jnp.float32)
        for q in range(ROWS):
            pivot = cols[q][q : q + 1]
            inv = 1.0 / pivot
            factor = jnp.where(sub > q, cols[q] * inv, 0.0)
            ahead = {r: cols[r][q : q + 1] for r in range(q + 1, ROWS)}
            for r in range(q + 1, ROWS):
                cols[r] = cols[r] - factor * ahead[r]
            row = head[q : q + 1]
            head = head - factor * row
            scale = jnp.where(sub == q, lax.rsqrt(pivot), scale)
            pivots.append(inv)
            crossed.append(ahead)
            kept.append(row)
        tiles[first] = head * scale
        for t in range(first + 1, n // ROWS):
            tile = tiles[t]
            cols_t = [jnp.broadcast_to(tile[:, start + q : start + q + 1], (ROWS, n)) for q in range(ROWS)]
            tile = jnp.where(inside, 0.0, tile)
            for q in range(ROWS):
                factor = cols_t[q] * pivots[q]
                for r in range(q + 1, ROWS):
                    cols_t[r] = cols_t[r] - factor * crossed[q][r]
                tile = tile - factor * kept[q]
            tiles[t] = tile
    out = jnp.concatenate(tiles, axis=0)
    rows_id = lax.broadcasted_iota(jnp.int32, (n, n), 0)
    cols_id = lax.broadcasted_iota(jnp.int32, (n, n), 1)
    return jnp.where(rows_id >= cols_id, out, 0.0)


def orthonormal_kernel(count, gram_ref, upper_ref, growth_ref, work):
    n = gram_ref.shape[0]
    work[...] = gram_ref[...] * (1.0 / count)
    cols_id = lax.broadcasted_iota(jnp.int32, (NB, n), 1)

    def step(i, carry):
        at = pl.multiple_of(i * NB, NB)
        diag = inverse_factor(work[pl.ds(at, NB), pl.ds(at, NB)])
        work[:, pl.ds(at, NB)] = jnp.zeros((n, NB), jnp.float32)
        rows = jnp.dot(diag, work[pl.ds(at, NB), :], precision=HI, preferred_element_type=jnp.float32)
        work[pl.ds(at, NB), :] = rows
        work[pl.ds(at, NB), pl.ds(at, NB)] = diag
        rows = work[pl.ds(at, NB), :]
        panel = jnp.where(cols_id >= at + NB, rows, 0.0)
        work[...] -= lax.dot_general(
            panel, rows, (((0,), (0,)), ((), ())), precision=HI, preferred_element_type=jnp.float32
        )
        return carry

    lax.fori_loop(0, n // NB, step, 0)
    rows_n = lax.broadcasted_iota(jnp.int32, (n, n), 0)
    cols_n = lax.broadcasted_iota(jnp.int32, (n, n), 1)
    full = work[...]
    upper_ref[...] = jnp.where(rows_n >= cols_n, full, 0.0).T.astype(jnp.bfloat16)
    growth_ref[...] = -jnp.log(jnp.sum(jnp.where(rows_n == cols_n, full, 0.0), axis=0, keepdims=True))


def orthonormalize(gram_total, count):
    n = gram_total.shape[0]
    upper, growth = pl.pallas_call(
        functools.partial(orthonormal_kernel, count),
        out_shape=(
            jax.ShapeDtypeStruct((n, n), jnp.bfloat16),
            jax.ShapeDtypeStruct((1, n), jnp.float32),
        ),
        in_specs=[pl.BlockSpec(memory_space=pltpu.VMEM)],
        out_specs=(pl.BlockSpec(memory_space=pltpu.VMEM), pl.BlockSpec(memory_space=pltpu.VMEM)),
        scratch_shapes=[pltpu.VMEM((n, n), jnp.float32)],
        compiler_params=pltpu.CompilerParams(vmem_limit_bytes=32 * 1024 * 1024),
        name="orthonormalize",
    )(gram_total)
    return upper, growth[0]


def gain_slope(volt_now):
    sigma_value = jax.nn.sigmoid((volt_now - THRESHOLD) / SIGMOID_WIDTH)
    return sigma_value * (1.0 - sigma_value) / SIGMOID_WIDTH


def shifted(value, axis, step, closed):
    count = lax.axis_size(axis)
    pairs = [(i, i + step) for i in range(count)]
    if closed:
        pairs = [(i, j % count) for i, j in pairs]
    else:
        pairs = [(i, j) for i, j in pairs if 0 <= j < count]
    return lax.ppermute(value, axis, pairs)


def neighbours(cells):
    before = shifted(cells[-2:], "col", 1, True)
    after = shifted(cells[:2], "col", -1, True)
    above = shifted(cells, "layer", 1, False)
    below = shifted(cells, "layer", -1, False)
    return before, after, above, below


def exchanged(value):
    return lax.all_to_all(value, "col", split_axis=0, concat_axis=0, tiled=True)


def advance_kernel(
    per_step, tangents_ref, before_ref, own_ref, after_ref, above_ref, below_ref, far_ref,
    weights_ref, far_weights_ref, coef_ref, advanced_ref, gram_ref, wide
):
    index = pl.program_id(0)
    blocks, size, _ = own_ref.shape

    @pl.when(index == 0)
    def _():
        wide[0:2] = before_ref[...]
        wide[2 : 2 + blocks] = own_ref[...]
        wide[2 + blocks : 4 + blocks] = after_ref[...]
        gram_ref[...] = jnp.zeros_like(gram_ref)

    for k in range(per_step):
        at = index * per_step + k
        coef = coef_ref[k]

        def times(weight, source):
            return jnp.dot(weight, source, preferred_element_type=jnp.float32)

        drive = coef[:, 7:8] * times(far_weights_ref[k], far_ref[...])
        for j in range(5):
            drive += coef[:, j : j + 1] * times(weights_ref[k, j], wide[at + j])
        drive += coef[:, 5:6] * times(weights_ref[k, 5], above_ref[at])
        drive += coef[:, 6:7] * times(weights_ref[k, 6], below_ref[at])
        now = tangents_ref[k].astype(jnp.float32)
        advanced_ref[k] = (now + TIME_STEP * (drive - coef[:, 8:9] * now)).astype(jnp.bfloat16)
    rows = advanced_ref[...].reshape(per_step * size, advanced_ref.shape[-1])
    gram_ref[...] += lax.dot_general(
        rows, rows, (((0,), (0,)), ((), ())), preferred_element_type=jnp.float32
    )


def advance(tangents, before, own, after, above, below, far, weights, far_weights, coef):
    blocks, size, vectors = tangents.shape
    per_step = 2 if blocks % 2 == 0 else 1
    whole = pl.BlockSpec(memory_space=pltpu.VMEM)

    def split(*rest):
        return pl.BlockSpec((per_step,) + rest, lambda i: (i,) + (0,) * len(rest))

    return pl.pallas_call(
        functools.partial(advance_kernel, per_step),
        grid=(blocks // per_step,),
        out_shape=(
            jax.ShapeDtypeStruct(tangents.shape, jnp.bfloat16),
            jax.ShapeDtypeStruct((vectors, vectors), jnp.float32),
        ),
        in_specs=[
            split(size, vectors),
            whole, whole, whole, whole, whole, whole,
            split(7, size, size),
            split(size, far.shape[0]),
            split(size, coef.shape[-1]),
        ],
        out_specs=(split(size, vectors), pl.BlockSpec((vectors, vectors), lambda i: (0, 0))),
        scratch_shapes=[pltpu.VMEM((blocks + 4, size, vectors), jnp.bfloat16)],
        compiler_params=pltpu.CompilerParams(
            vmem_limit_bytes=48 * 1024 * 1024, dimension_semantics=("arbitrary",)
        ),
        name="advance",
    )(tangents, before, own, after, above, below, far, weights, far_weights, coef)


def body(
    tangents,
    voltage,
    conductance,
    local_weights,
    block_label,
    pair_dest,
    pair_target,
    bundle_source,
    pair_weights,
):
    lay_blocks, col_blocks, size, vectors = tangents.shape
    steps = voltage.shape[0]
    blocks = col_blocks
    col_count = lax.axis_size("col")
    lay_count = lax.axis_size("layer")
    destination = pair_dest[0, 0, :, 0]
    target_block = pair_target[0, 0]
    bundle_row = bundle_source[0, 0]
    pair_count = destination.shape[0]
    capacity = max(2, 2 * pair_count // col_count)
    slot_count = col_count * capacity
    neurons = float(blocks * size * col_count * lay_count)
    layer = lax.axis_index("layer")
    col_start = lax.axis_index("col") * blocks

    pair_order = jnp.arange(pair_count, dtype=jnp.int32)
    earlier = (destination[:, None] == destination[None, :]) & (
        pair_order[None, :] < pair_order[:, None]
    )
    slot_index = destination * capacity + jnp.sum(earlier.astype(jnp.int32), axis=1)
    placement = jnp.arange(slot_count, dtype=jnp.int32)[:, None] == slot_index[None, :]
    slot_target = jnp.sum(jnp.where(placement, target_block[None, :], 0), axis=1)
    slot_weights = jnp.dot(
        placement.astype(jnp.bfloat16),
        pair_weights[0, 0].reshape(pair_count, size * size),
        preferred_element_type=jnp.float32,
    ).astype(jnp.bfloat16)
    bundle_pick = (
        bundle_row[:, None] == jnp.arange(blocks, dtype=jnp.int32)[None, :]
    )

    def bundle(cells):
        picked = jnp.dot(
            bundle_pick.astype(jnp.bfloat16), cells.reshape(blocks, -1),
            preferred_element_type=jnp.float32,
        )
        return picked.astype(jnp.bfloat16).reshape(col_count, size, vectors)

    volt = voltage[:, 0]
    slope = gain_slope(volt)
    state = tangents[0]
    scaled = (state * slope[0][..., None]).astype(jnp.bfloat16)
    edges = neighbours(scaled)
    far = exchanged(bundle(scaled))
    got_weights = exchanged(slot_weights.reshape(col_count, capacity, size * size))
    got_target = exchanged(slot_target.astype(jnp.int32).reshape(col_count, 1, capacity))
    bundle_slope = jnp.sum(jnp.where(bundle_pick[:, :, None, None], slope.transpose(1, 0, 2)[None], 0.0), axis=1)
    far_slope = exchanged(bundle_slope)
    edge_slope = [
        edge.transpose(1, 0, 2) for edge in neighbours(slope.transpose(1, 0, 2))
    ]
    hit = (
        got_target.reshape(col_count, 1, capacity)
        == jnp.arange(blocks, dtype=jnp.int32)[None, :, None]
    ).astype(jnp.bfloat16)
    far_weights = (
        lax.dot_general(
            hit, got_weights, (((2,), (1,)), ((0,), (0,))), preferred_element_type=jnp.float32
        )
        .astype(jnp.bfloat16)
        .reshape(col_count, blocks, size, size)
        .transpose(1, 2, 0, 3)
        .reshape(blocks, size, col_count * size)
    )

    reversal = jnp.where(block_label == 1, INHIBIT_REVERSAL, EXCITE_REVERSAL).astype(jnp.float32)
    edge_row = jnp.full((1, reversal.shape[1]), EXCITE_REVERSAL, jnp.float32)
    reversal = jnp.concatenate([edge_row, reversal, edge_row], axis=0)
    reversal = jnp.concatenate([reversal[:, -2:], reversal, reversal[:, :2]], axis=1)
    near = lax.dynamic_slice(reversal, (layer, col_start), (3, blocks + 4))
    potential = jnp.stack(
        [near[1, j : j + blocks] for j in range(5)]
        + [near[0, 2 : 2 + blocks], near[2, 2 : 2 + blocks], jnp.full((blocks,), EXCITE_REVERSAL)],
        axis=-1,
    )

    growth = jnp.zeros((vectors,), jnp.float32)
    for t in range(steps):
        coef = jnp.concatenate(
            [
                potential[:, None, :] - volt[t][..., None],
                conductance[t, 0][..., None],
                jnp.zeros((blocks, size, 7), jnp.float32),
            ],
            axis=-1,
        )
        advanced, gram = advance(
            state, edges[0], scaled, edges[1], edges[2], edges[3],
            far.reshape(col_count * size, vectors), local_weights[0], far_weights, coef,
        )
        gram = lax.psum(gram, ("col", "layer"))
        last = t == steps - 1
        if not last:
            edges = neighbours(advanced)
            far = exchanged(bundle(advanced))
        upper, grown = orthonormalize(gram, neurons)
        growth = growth + grown

        def rotated(cells):
            return jnp.dot(cells, upper, preferred_element_type=jnp.float32).astype(jnp.bfloat16)

        state = rotated(advanced)
        if not last:
            scaled = (state * slope[t + 1][..., None]).astype(jnp.bfloat16)
            edges = [
                (rotated(edge) * edge_slope[k][t + 1][..., None]).astype(jnp.bfloat16)
                for k, edge in enumerate(edges)
            ]
            far = (rotated(far) * far_slope[:, t + 1, :, None]).astype(jnp.bfloat16)
    return state[None], growth


def solution(mesh):
    in_specs = (
        P("layer", "col", None, None),
        P(None, "layer", "col", None),
        P(None, "layer", "col", None),
        P("layer", "col", None, None, None),
        P(),
        P("layer", "col", None, None),
        P("layer", "col", None),
        P("layer", "col", None),
        P("layer", "col", None, None, None),
    )
    out_specs = (P("layer", "col", None, None), P())
    return jax.shard_map(body, mesh=mesh, in_specs=in_specs, out_specs=out_specs, check_vma=False)
```

```python
import functools

import jax
import jax.numpy as jnp
from jax import lax
from jax.experimental import pallas as pl
from jax.experimental.pallas import tpu as pltpu
from jax.sharding import PartitionSpec as P

EXCITE_REVERSAL = 1.0
INHIBIT_REVERSAL = -0.5
THRESHOLD = 0.2
SIGMOID_WIDTH = 0.1
TIME_STEP = 0.1
HI = lax.Precision.HIGHEST
NB = 128
ROWS = 8
MESH = pl.DeviceIdType.MESH
LANES = 128


def half_rows(vectors, chunks):
    count = -(-vectors // LANES)
    rows = -(-(count * (count + 1) // 2) // 2) * LANES
    return -(-rows // (8 * chunks)) * 8 * chunks


def packed_places(vectors, half):
    count = -(-vectors // LANES)
    pairs = [(i, j) for i in range(count) for j in range(i + 1)]
    each = -(-len(pairs) // 2)
    return [(i, j, (k // each) * half + (k % each) * LANES) for k, (i, j) in enumerate(pairs)]


def sum_kernel(groups, per_col, packed_ref, total_ref, mate_in, part, arrived, sems):
    chunk = part.shape[1]
    half = groups * chunk
    col, layer = lax.axis_index("col"), lax.axis_index("layer")
    core = lax.rem(layer, 2)
    mate = {"col": col, "layer": layer + 1 - 2 * core}
    me = col * per_col + layer // 2

    def peer(step):
        k = lax.rem(me + step, groups)
        return k, {"col": k // per_col, "layer": lax.rem(k, per_col) * 2 + core}

    def remote(source, target, kind, sent, got, device):
        return pltpu.make_async_remote_copy(
            src_ref=source,
            dst_ref=target,
            send_sem=sems.at[kind, sent],
            recv_sem=sems.at[kind + 1, got],
            device_id=device,
            device_id_type=MESH,
        )

    barrier = pltpu.get_barrier_semaphore()
    pl.semaphore_signal(barrier, inc=1, device_id=mate, device_id_type=MESH)

    def greet(step, carry):
        _, device = peer(step)
        pl.semaphore_signal(barrier, inc=1, device_id=device, device_id_type=MESH)
        return carry

    lax.fori_loop(1, groups, greet, 0)
    pl.semaphore_wait(barrier, groups)

    mine = pl.multiple_of(core * half, 8)
    other = pl.multiple_of((1 - core) * half, 8)
    swap = remote(packed_ref.at[pl.ds(other, half)], mate_in, 6, 0, 0, mate)
    swap.start()
    swap.wait()
    part[...] = (packed_ref[pl.ds(mine, half), :] + mate_in[...]).reshape(part.shape)

    def scatter(step, carry):
        k, device = peer(step)
        remote(part.at[k], arrived.at[me], 0, k, me, device).start()
        return carry

    def scattered(step, carry):
        k, device = peer(step)
        copy = remote(part.at[k], arrived.at[k], 0, k, k, device)
        copy.wait_send()
        copy.wait_recv()
        return carry

    lax.fori_loop(1, groups, scatter, 0)
    arrived[me] = part[me]
    lax.fori_loop(1, groups, scattered, 0)

    def place(k):
        return total_ref.at[pl.ds(pl.multiple_of(core * half + k * chunk, 8), chunk)]

    def mate_place(k):
        return total_ref.at[pl.ds(pl.multiple_of((1 - core) * half + k * chunk, 8), chunk)]

    place(me)[...] = jnp.sum(arrived[...], axis=0)

    def spread(step, carry):
        k, device = peer(step)
        remote(place(me), place(me), 2, k, me, device).start()
        return carry

    def forward(step, carry):
        k, device = peer(step)
        copy = remote(place(me), place(k), 2, k, k, device)
        copy.wait_recv()
        remote(place(k), place(k), 4, k, k, mate).start()
        return carry

    def finish(step, carry):
        k, device = peer(step)
        remote(place(me), place(k), 2, k, k, device).wait_send()
        copy = remote(place(k), mate_place(k), 4, k, k, mate)
        copy.wait_send()
        copy.wait_recv()
        return carry

    lax.fori_loop(1, groups, spread, 0)
    own = remote(place(me), place(me), 4, me, me, mate)
    own.start()
    lax.fori_loop(1, groups, forward, 0)
    last = remote(place(me), mate_place(me), 4, me, me, mate)
    last.wait_send()
    last.wait_recv()
    lax.fori_loop(1, groups, finish, 0)


def summed(packed):
    per_col = lax.axis_size("layer") // 2
    groups = lax.axis_size("col") * per_col
    half = packed.shape[0] // 2
    chunk = half // groups
    return pl.pallas_call(
        functools.partial(sum_kernel, groups, per_col),
        out_shape=jax.ShapeDtypeStruct(packed.shape, packed.dtype),
        in_specs=[pl.BlockSpec(memory_space=pltpu.VMEM)],
        out_specs=pl.BlockSpec(memory_space=pltpu.VMEM),
        scratch_shapes=[
            pltpu.VMEM((half, LANES), packed.dtype),
            pltpu.VMEM((groups, chunk, LANES), packed.dtype),
            pltpu.VMEM((groups, chunk, LANES), packed.dtype),
            pltpu.SemaphoreType.DMA((8, groups)),
        ],
        compiler_params=pltpu.CompilerParams(
            collective_id=0, has_side_effects=True, vmem_limit_bytes=16 * 1024 * 1024
        ),
        name="sum_gram",
    )(packed)


def inverse_factor(block):
    n = block.shape[0]
    lane = lax.broadcasted_iota(jnp.int32, (ROWS, n), 1)
    sub = lax.broadcasted_iota(jnp.int32, (ROWS, n), 0)
    tiles = [block[t * ROWS : (t + 1) * ROWS] for t in range(n // ROWS)]
    for first in range(n // ROWS):
        start = first * ROWS
        inside = (lane >= start) & (lane < start + ROWS)
        head = tiles[first]
        cols = [jnp.broadcast_to(head[:, start + q : start + q + 1], (ROWS, n)) for q in range(ROWS)]
        head = jnp.where(lane == sub + start, 1.0, jnp.where(inside, 0.0, head))
        pivots, crossed, kept = [], [], []
        scale = jnp.zeros((ROWS, n), jnp.float32)
        for q in range(ROWS):
            pivot = cols[q][q : q + 1]
            inv = 1.0 / pivot
            factor = jnp.where(sub > q, cols[q] * inv, 0.0)
            ahead = {r: cols[r][q : q + 1] for r in range(q + 1, ROWS)}
            for r in range(q + 1, ROWS):
                cols[r] = cols[r] - factor * ahead[r]
            row = head[q : q + 1]
            head = head - factor * row
            scale = jnp.where(sub == q, lax.rsqrt(pivot), scale)
            pivots.append(inv)
            crossed.append(ahead)
            kept.append(row)
        tiles[first] = head * scale
        for t in range(first + 1, n // ROWS):
            tile = tiles[t]
            cols_t = [jnp.broadcast_to(tile[:, start + q : start + q + 1], (ROWS, n)) for q in range(ROWS)]
            tile = jnp.where(inside, 0.0, tile)
            for q in range(ROWS):
                factor = cols_t[q] * pivots[q]
                for r in range(q + 1, ROWS):
                    cols_t[r] = cols_t[r] - factor * crossed[q][r]
                tile = tile - factor * kept[q]
            tiles[t] = tile
    out = jnp.concatenate(tiles, axis=0)
    rows_id = lax.broadcasted_iota(jnp.int32, (n, n), 0)
    cols_id = lax.broadcasted_iota(jnp.int32, (n, n), 1)
    return jnp.where(rows_id >= cols_id, out, 0.0)


def orthonormal_kernel(count, packed_ref, upper_ref, growth_ref, work):
    n = upper_ref.shape[0]
    for i, j, at in packed_places(n, packed_ref.shape[0] // 2):
        block = packed_ref[at : at + LANES] * (1.0 / count)
        work[i * LANES : (i + 1) * LANES, j * LANES : (j + 1) * LANES] = block
        if i > j:
            work[j * LANES : (j + 1) * LANES, i * LANES : (i + 1) * LANES] = block.T
    cols_id = lax.broadcasted_iota(jnp.int32, (NB, n), 1)

    def step(i, carry):
        at = pl.multiple_of(i * NB, NB)
        diag = inverse_factor(work[pl.ds(at, NB), pl.ds(at, NB)])
        work[:, pl.ds(at, NB)] = jnp.zeros((n, NB), jnp.float32)
        rows = jnp.dot(diag, work[pl.ds(at, NB), :], precision=HI, preferred_element_type=jnp.float32)
        work[pl.ds(at, NB), :] = rows
        work[pl.ds(at, NB), pl.ds(at, NB)] = diag
        rows = work[pl.ds(at, NB), :]
        panel = jnp.where(cols_id >= at + NB, rows, 0.0)
        work[...] -= lax.dot_general(
            panel, rows, (((0,), (0,)), ((), ())), precision=HI, preferred_element_type=jnp.float32
        )
        return carry

    lax.fori_loop(0, n // NB, step, 0)
    rows_n = lax.broadcasted_iota(jnp.int32, (n, n), 0)
    cols_n = lax.broadcasted_iota(jnp.int32, (n, n), 1)
    full = work[...]
    upper_ref[...] = jnp.where(rows_n >= cols_n, full, 0.0).T.astype(jnp.bfloat16)
    growth_ref[...] = -jnp.log(jnp.sum(jnp.where(rows_n == cols_n, full, 0.0), axis=0, keepdims=True))


def orthonormalize(gram_total, count, n):
    upper, growth = pl.pallas_call(
        functools.partial(orthonormal_kernel, count),
        out_shape=(
            jax.ShapeDtypeStruct((n, n), jnp.bfloat16),
            jax.ShapeDtypeStruct((1, n), jnp.float32),
        ),
        in_specs=[pl.BlockSpec(memory_space=pltpu.VMEM)],
        out_specs=(pl.BlockSpec(memory_space=pltpu.VMEM), pl.BlockSpec(memory_space=pltpu.VMEM)),
        scratch_shapes=[pltpu.VMEM((n, n), jnp.float32)],
        compiler_params=pltpu.CompilerParams(vmem_limit_bytes=32 * 1024 * 1024),
        name="orthonormalize",
    )(gram_total)
    return upper, growth[0]


def gain_slope(volt_now):
    sigma_value = jax.nn.sigmoid((volt_now - THRESHOLD) / SIGMOID_WIDTH)
    return sigma_value * (1.0 - sigma_value) / SIGMOID_WIDTH


def shifted(value, axis, step, closed):
    count = lax.axis_size(axis)
    pairs = [(i, i + step) for i in range(count)]
    if closed:
        pairs = [(i, j % count) for i, j in pairs]
    else:
        pairs = [(i, j) for i, j in pairs if 0 <= j < count]
    return lax.ppermute(value, axis, pairs)


def neighbours(cells):
    before = shifted(cells[-2:], "col", 1, True)
    after = shifted(cells[:2], "col", -1, True)
    above = shifted(cells, "layer", 1, False)
    below = shifted(cells, "layer", -1, False)
    return before, after, above, below


def exchanged(value):
    return lax.all_to_all(value, "col", split_axis=0, concat_axis=0, tiled=True)


def advance_kernel(
    per_step, tangents_ref, before_ref, own_ref, after_ref, above_ref, below_ref, far_ref,
    weights_ref, far_weights_ref, coef_ref, advanced_ref, gram_ref, wide, total
):
    index = pl.program_id(0)
    blocks, size, _ = own_ref.shape

    @pl.when(index == 0)
    def _():
        wide[0:2] = before_ref[...]
        wide[2 : 2 + blocks] = own_ref[...]
        wide[2 + blocks : 4 + blocks] = after_ref[...]
        total[...] = jnp.zeros_like(total)

    for k in range(per_step):
        at = index * per_step + k
        coef = coef_ref[k]

        def times(weight, source):
            return jnp.dot(weight, source, preferred_element_type=jnp.float32)

        drive = coef[:, 7:8] * times(far_weights_ref[k], far_ref[...])
        for j in range(5):
            drive += coef[:, j : j + 1] * times(weights_ref[k, j], wide[at + j])
        drive += coef[:, 5:6] * times(weights_ref[k, 5], above_ref[at])
        drive += coef[:, 6:7] * times(weights_ref[k, 6], below_ref[at])
        now = tangents_ref[k].astype(jnp.float32)
        advanced_ref[k] = (now + TIME_STEP * (drive - coef[:, 8:9] * now)).astype(jnp.bfloat16)
    rows = advanced_ref[...].reshape(per_step * size, advanced_ref.shape[-1])
    total[...] += lax.dot_general(
        rows, rows, (((0,), (0,)), ((), ())), preferred_element_type=jnp.float32
    )

    @pl.when(index == pl.num_programs(0) - 1)
    def _():
        gram_ref[...] = jnp.zeros_like(gram_ref)
        for i, j, at in packed_places(total.shape[0], gram_ref.shape[0] // 2):
            gram_ref[at : at + LANES] = total[
                i * LANES : (i + 1) * LANES, j * LANES : (j + 1) * LANES
            ]


def advance(tangents, before, own, after, above, below, far, weights, far_weights, coef):
    blocks, size, vectors = tangents.shape
    half = half_rows(vectors, lax.axis_size("col") * lax.axis_size("layer") // 2)
    per_step = 2 if blocks % 2 == 0 else 1
    whole = pl.BlockSpec(memory_space=pltpu.VMEM)

    def split(*rest):
        return pl.BlockSpec((per_step,) + rest, lambda i: (i,) + (0,) * len(rest))

    return pl.pallas_call(
        functools.partial(advance_kernel, per_step),
        grid=(blocks // per_step,),
        out_shape=(
            jax.ShapeDtypeStruct(tangents.shape, jnp.bfloat16),
            jax.ShapeDtypeStruct((2 * half, LANES), jnp.float32),
        ),
        in_specs=[
            split(size, vectors),
            whole, whole, whole, whole, whole, whole,
            split(7, size, size),
            split(size, far.shape[0]),
            split(size, coef.shape[-1]),
        ],
        out_specs=(split(size, vectors), pl.BlockSpec((2 * half, LANES), lambda i: (0, 0))),
        scratch_shapes=[
            pltpu.VMEM((blocks + 4, size, vectors), jnp.bfloat16),
            pltpu.VMEM((vectors, vectors), jnp.float32),
        ],
        compiler_params=pltpu.CompilerParams(
            vmem_limit_bytes=48 * 1024 * 1024, dimension_semantics=("arbitrary",)
        ),
        name="advance",
    )(tangents, before, own, after, above, below, far, weights, far_weights, coef)


def body(
    tangents,
    voltage,
    conductance,
    local_weights,
    block_label,
    pair_dest,
    pair_target,
    bundle_source,
    pair_weights,
):
    lay_blocks, col_blocks, size, vectors = tangents.shape
    steps = voltage.shape[0]
    blocks = col_blocks
    col_count = lax.axis_size("col")
    lay_count = lax.axis_size("layer")
    destination = pair_dest[0, 0, :, 0]
    target_block = pair_target[0, 0]
    bundle_row = bundle_source[0, 0]
    pair_count = destination.shape[0]
    capacity = max(2, 2 * pair_count // col_count)
    slot_count = col_count * capacity
    neurons = float(blocks * size * col_count * lay_count)
    layer = lax.axis_index("layer")
    col_start = lax.axis_index("col") * blocks

    pair_order = jnp.arange(pair_count, dtype=jnp.int32)
    earlier = (destination[:, None] == destination[None, :]) & (
        pair_order[None, :] < pair_order[:, None]
    )
    slot_index = destination * capacity + jnp.sum(earlier.astype(jnp.int32), axis=1)
    placement = jnp.arange(slot_count, dtype=jnp.int32)[:, None] == slot_index[None, :]
    slot_target = jnp.sum(jnp.where(placement, target_block[None, :], 0), axis=1)
    slot_weights = jnp.dot(
        placement.astype(jnp.bfloat16),
        pair_weights[0, 0].reshape(pair_count, size * size),
        preferred_element_type=jnp.float32,
    ).astype(jnp.bfloat16)
    bundle_pick = (
        bundle_row[:, None] == jnp.arange(blocks, dtype=jnp.int32)[None, :]
    )

    def bundle(cells):
        picked = jnp.dot(
            bundle_pick.astype(jnp.bfloat16), cells.reshape(blocks, -1),
            preferred_element_type=jnp.float32,
        )
        return picked.astype(jnp.bfloat16).reshape(col_count, size, vectors)

    volt = voltage[:, 0]
    slope = gain_slope(volt)
    state = tangents[0]
    scaled = (state * slope[0][..., None]).astype(jnp.bfloat16)
    edges = neighbours(scaled)
    far = exchanged(bundle(scaled))
    got_weights = exchanged(slot_weights.reshape(col_count, capacity, size * size))
    got_target = exchanged(slot_target.astype(jnp.int32).reshape(col_count, 1, capacity))
    bundle_slope = jnp.sum(jnp.where(bundle_pick[:, :, None, None], slope.transpose(1, 0, 2)[None], 0.0), axis=1)
    far_slope = exchanged(bundle_slope)
    edge_slope = [
        edge.transpose(1, 0, 2) for edge in neighbours(slope.transpose(1, 0, 2))
    ]
    hit = (
        got_target.reshape(col_count, 1, capacity)
        == jnp.arange(blocks, dtype=jnp.int32)[None, :, None]
    ).astype(jnp.bfloat16)
    far_weights = (
        lax.dot_general(
            hit, got_weights, (((2,), (1,)), ((0,), (0,))), preferred_element_type=jnp.float32
        )
        .astype(jnp.bfloat16)
        .reshape(col_count, blocks, size, size)
        .transpose(1, 2, 0, 3)
        .reshape(blocks, size, col_count * size)
    )

    reversal = jnp.where(block_label == 1, INHIBIT_REVERSAL, EXCITE_REVERSAL).astype(jnp.float32)
    edge_row = jnp.full((1, reversal.shape[1]), EXCITE_REVERSAL, jnp.float32)
    reversal = jnp.concatenate([edge_row, reversal, edge_row], axis=0)
    reversal = jnp.concatenate([reversal[:, -2:], reversal, reversal[:, :2]], axis=1)
    near = lax.dynamic_slice(reversal, (layer, col_start), (3, blocks + 4))
    potential = jnp.stack(
        [near[1, j : j + blocks] for j in range(5)]
        + [near[0, 2 : 2 + blocks], near[2, 2 : 2 + blocks], jnp.full((blocks,), EXCITE_REVERSAL)],
        axis=-1,
    )

    growth = jnp.zeros((vectors,), jnp.float32)
    for t in range(steps):
        coef = jnp.concatenate(
            [
                potential[:, None, :] - volt[t][..., None],
                conductance[t, 0][..., None],
                jnp.zeros((blocks, size, 7), jnp.float32),
            ],
            axis=-1,
        )
        advanced, gram = advance(
            state, edges[0], scaled, edges[1], edges[2], edges[3],
            far.reshape(col_count * size, vectors), local_weights[0], far_weights, coef,
        )
        gram = summed(gram)
        last = t == steps - 1
        if not last:
            edges = neighbours(advanced)
            far = exchanged(bundle(advanced))
        upper, grown = orthonormalize(gram, neurons, vectors)
        growth = growth + grown

        def rotated(cells):
            return jnp.dot(cells, upper, preferred_element_type=jnp.float32).astype(jnp.bfloat16)

        state = rotated(advanced)
        if not last:
            scaled = (state * slope[t + 1][..., None]).astype(jnp.bfloat16)
            edges = [
                (rotated(edge) * edge_slope[k][t + 1][..., None]).astype(jnp.bfloat16)
                for k, edge in enumerate(edges)
            ]
            far = (rotated(far) * far_slope[:, t + 1, :, None]).astype(jnp.bfloat16)
    return state[None], growth


def solution(mesh):
    in_specs = (
        P("layer", "col", None, None),
        P(None, "layer", "col", None),
        P(None, "layer", "col", None),
        P("layer", "col", None, None, None),
        P(),
        P("layer", "col", None, None),
        P("layer", "col", None),
        P("layer", "col", None),
        P("layer", "col", None, None, None),
    )
    out_specs = (P("layer", "col", None, None), P())
    return jax.shard_map(body, mesh=mesh, in_specs=in_specs, out_specs=out_specs, check_vma=False)
```

```python
import functools

import jax
import jax.numpy as jnp
from jax import lax
from jax.experimental import pallas as pl
from jax.experimental.pallas import tpu as pltpu
from jax.sharding import PartitionSpec as P

EXCITE_REVERSAL = 1.0
INHIBIT_REVERSAL = -0.5
THRESHOLD = 0.2
SIGMOID_WIDTH = 0.1
TIME_STEP = 0.1
HI = lax.Precision.HIGHEST
NB = 128
ROWS = 8
MESH = pl.DeviceIdType.MESH
LANES = 128


def half_rows(vectors, chunks):
    count = -(-vectors // LANES)
    rows = -(-(count * (count + 1) // 2) // 2) * LANES
    return -(-rows // (8 * chunks)) * 8 * chunks


def packed_places(vectors, half):
    count = -(-vectors // LANES)
    pairs = [(i, j) for i in range(count) for j in range(i + 1)]
    each = -(-len(pairs) // 2)
    return [(i, j, (k // each) * half + (k % each) * LANES) for k, (i, j) in enumerate(pairs)]


def sum_kernel(groups, per_col, packed_ref, total_ref, mate_in, part, arrived, sems):
    chunk = part.shape[1]
    half = groups * chunk
    col, layer = lax.axis_index("col"), lax.axis_index("layer")
    core = lax.rem(layer, 2)
    mate = {"col": col, "layer": layer + 1 - 2 * core}
    me = col * per_col + layer // 2

    def peer(step):
        k = lax.rem(me + step, groups)
        return k, {"col": k // per_col, "layer": lax.rem(k, per_col) * 2 + core}

    def remote(source, target, kind, sent, got, device):
        return pltpu.make_async_remote_copy(
            src_ref=source,
            dst_ref=target,
            send_sem=sems.at[kind, sent],
            recv_sem=sems.at[kind + 1, got],
            device_id=device,
            device_id_type=MESH,
        )

    barrier = pltpu.get_barrier_semaphore()
    pl.semaphore_signal(barrier, inc=1, device_id=mate, device_id_type=MESH)

    def greet(step, carry):
        _, device = peer(step)
        pl.semaphore_signal(barrier, inc=1, device_id=device, device_id_type=MESH)
        return carry

    lax.fori_loop(1, groups, greet, 0)
    pl.semaphore_wait(barrier, groups)

    mine = pl.multiple_of(core * half, 8)
    other = pl.multiple_of((1 - core) * half, 8)
    swap = remote(packed_ref.at[pl.ds(other, half)], mate_in, 6, 0, 0, mate)
    swap.start()
    swap.wait()
    part[...] = (packed_ref[pl.ds(mine, half), :] + mate_in[...]).reshape(part.shape)

    def scatter(step, carry):
        k, device = peer(step)
        remote(part.at[k], arrived.at[me], 0, k, me, device).start()
        return carry

    def scattered(step, carry):
        k, device = peer(step)
        copy = remote(part.at[k], arrived.at[k], 0, k, k, device)
        copy.wait_send()
        copy.wait_recv()
        return carry

    lax.fori_loop(1, groups, scatter, 0)
    arrived[me] = part[me]
    lax.fori_loop(1, groups, scattered, 0)

    def place(k):
        return total_ref.at[pl.ds(pl.multiple_of(core * half + k * chunk, 8), chunk)]

    def mate_place(k):
        return total_ref.at[pl.ds(pl.multiple_of((1 - core) * half + k * chunk, 8), chunk)]

    place(me)[...] = jnp.sum(arrived[...], axis=0)

    def spread(step, carry):
        k, device = peer(step)
        remote(place(me), place(me), 2, k, me, device).start()
        return carry

    def forward(step, carry):
        k, device = peer(step)
        copy = remote(place(me), place(k), 2, k, k, device)
        copy.wait_recv()
        remote(place(k), place(k), 4, k, k, mate).start()
        return carry

    def finish(step, carry):
        k, device = peer(step)
        remote(place(me), place(k), 2, k, k, device).wait_send()
        copy = remote(place(k), mate_place(k), 4, k, k, mate)
        copy.wait_send()
        copy.wait_recv()
        return carry

    lax.fori_loop(1, groups, spread, 0)
    own = remote(place(me), place(me), 4, me, me, mate)
    own.start()
    lax.fori_loop(1, groups, forward, 0)
    last = remote(place(me), mate_place(me), 4, me, me, mate)
    last.wait_send()
    last.wait_recv()
    lax.fori_loop(1, groups, finish, 0)


def summed(packed):
    per_col = lax.axis_size("layer") // 2
    groups = lax.axis_size("col") * per_col
    half = packed.shape[0] // 2
    chunk = half // groups
    return pl.pallas_call(
        functools.partial(sum_kernel, groups, per_col),
        out_shape=jax.ShapeDtypeStruct(packed.shape, packed.dtype),
        in_specs=[pl.BlockSpec(memory_space=pltpu.VMEM)],
        out_specs=pl.BlockSpec(memory_space=pltpu.VMEM),
        scratch_shapes=[
            pltpu.VMEM((half, LANES), packed.dtype),
            pltpu.VMEM((groups, chunk, LANES), packed.dtype),
            pltpu.VMEM((groups, chunk, LANES), packed.dtype),
            pltpu.SemaphoreType.DMA((8, groups)),
        ],
        compiler_params=pltpu.CompilerParams(
            collective_id=0, has_side_effects=True, vmem_limit_bytes=16 * 1024 * 1024
        ),
        name="sum_gram",
    )(packed)


def inverse_factor(block):
    n = block.shape[0]
    lane = lax.broadcasted_iota(jnp.int32, (ROWS, n), 1)
    sub = lax.broadcasted_iota(jnp.int32, (ROWS, n), 0)
    tiles = [block[t * ROWS : (t + 1) * ROWS] for t in range(n // ROWS)]
    for first in range(n // ROWS):
        start = first * ROWS
        inside = (lane >= start) & (lane < start + ROWS)
        head = tiles[first]
        cols = [jnp.broadcast_to(head[:, start + q : start + q + 1], (ROWS, n)) for q in range(ROWS)]
        head = jnp.where(lane == sub + start, 1.0, jnp.where(inside, 0.0, head))
        pivots, crossed, kept = [], [], []
        scale = jnp.zeros((ROWS, n), jnp.float32)
        for q in range(ROWS):
            pivot = cols[q][q : q + 1]
            inv = 1.0 / pivot
            factor = jnp.where(sub > q, cols[q] * inv, 0.0)
            ahead = {r: cols[r][q : q + 1] for r in range(q + 1, ROWS)}
            for r in range(q + 1, ROWS):
                cols[r] = cols[r] - factor * ahead[r]
            row = head[q : q + 1]
            head = head - factor * row
            scale = jnp.where(sub == q, lax.rsqrt(pivot), scale)
            pivots.append(inv)
            crossed.append(ahead)
            kept.append(row)
        tiles[first] = head * scale
        for t in range(first + 1, n // ROWS):
            tile = tiles[t]
            cols_t = [jnp.broadcast_to(tile[:, start + q : start + q + 1], (ROWS, n)) for q in range(ROWS)]
            tile = jnp.where(inside, 0.0, tile)
            for q in range(ROWS):
                factor = cols_t[q] * pivots[q]
                for r in range(q + 1, ROWS):
                    cols_t[r] = cols_t[r] - factor * crossed[q][r]
                tile = tile - factor * kept[q]
            tiles[t] = tile
    out = jnp.concatenate(tiles, axis=0)
    rows_id = lax.broadcasted_iota(jnp.int32, (n, n), 0)
    cols_id = lax.broadcasted_iota(jnp.int32, (n, n), 1)
    return jnp.where(rows_id >= cols_id, out, 0.0)


def orthonormal_kernel(count, packed_ref, upper_ref, growth_ref, work):
    n = upper_ref.shape[0]
    for i, j, at in packed_places(n, packed_ref.shape[0] // 2):
        block = packed_ref[at : at + LANES] * (1.0 / count)
        work[i * LANES : (i + 1) * LANES, j * LANES : (j + 1) * LANES] = block
        if i > j:
            work[j * LANES : (j + 1) * LANES, i * LANES : (i + 1) * LANES] = block.T
    cols_id = lax.broadcasted_iota(jnp.int32, (NB, n), 1)

    def step(i, carry):
        at = pl.multiple_of(i * NB, NB)
        diag = inverse_factor(work[pl.ds(at, NB), pl.ds(at, NB)])
        work[:, pl.ds(at, NB)] = jnp.zeros((n, NB), jnp.float32)
        rows = jnp.dot(diag, work[pl.ds(at, NB), :], precision=HI, preferred_element_type=jnp.float32)
        work[pl.ds(at, NB), :] = rows
        work[pl.ds(at, NB), pl.ds(at, NB)] = diag
        rows = work[pl.ds(at, NB), :]
        panel = jnp.where(cols_id >= at + NB, rows, 0.0)
        work[...] -= lax.dot_general(
            panel, rows, (((0,), (0,)), ((), ())), precision=HI, preferred_element_type=jnp.float32
        )
        return carry

    lax.fori_loop(0, n // NB, step, 0)
    rows_n = lax.broadcasted_iota(jnp.int32, (n, n), 0)
    cols_n = lax.broadcasted_iota(jnp.int32, (n, n), 1)
    full = work[...]
    upper_ref[...] = jnp.where(rows_n >= cols_n, full, 0.0).T.astype(jnp.bfloat16)
    growth_ref[...] = -jnp.log(jnp.sum(jnp.where(rows_n == cols_n, full, 0.0), axis=0, keepdims=True))


def orthonormalize(gram_total, count, n):
    upper, growth = pl.pallas_call(
        functools.partial(orthonormal_kernel, count),
        out_shape=(
            jax.ShapeDtypeStruct((n, n), jnp.bfloat16),
            jax.ShapeDtypeStruct((1, n), jnp.float32),
        ),
        in_specs=[pl.BlockSpec(memory_space=pltpu.VMEM)],
        out_specs=(pl.BlockSpec(memory_space=pltpu.VMEM), pl.BlockSpec(memory_space=pltpu.VMEM)),
        scratch_shapes=[pltpu.VMEM((n, n), jnp.float32)],
        compiler_params=pltpu.CompilerParams(vmem_limit_bytes=16 * 1024 * 1024),
        cost_estimate=pl.CostEstimate(flops=30_000_000_000, bytes_accessed=90_000_000, transcendentals=n),
        name="orthonormalize",
    )(gram_total)
    return upper, growth[0]


def gain_slope(volt_now):
    sigma_value = jax.nn.sigmoid((volt_now - THRESHOLD) / SIGMOID_WIDTH)
    return sigma_value * (1.0 - sigma_value) / SIGMOID_WIDTH


def shifted(value, axis, step, closed):
    count = lax.axis_size(axis)
    pairs = [(i, i + step) for i in range(count)]
    if closed:
        pairs = [(i, j % count) for i, j in pairs]
    else:
        pairs = [(i, j) for i, j in pairs if 0 <= j < count]
    return lax.ppermute(value, axis, pairs)


def neighbours(cells):
    before = shifted(cells[-2:], "col", 1, True)
    after = shifted(cells[:2], "col", -1, True)
    above = shifted(cells, "layer", 1, False)
    below = shifted(cells, "layer", -1, False)
    return before, after, above, below


def exchanged(value):
    return lax.all_to_all(value, "col", split_axis=0, concat_axis=0, tiled=True)


def advance_kernel(
    per_step, tangents_ref, before_ref, own_ref, after_ref, above_ref, below_ref, far_ref,
    weights_ref, far_weights_ref, coef_ref, advanced_ref, gram_ref, wide, total
):
    index = pl.program_id(0)
    blocks, size, _ = own_ref.shape

    @pl.when(index == 0)
    def _():
        wide[0:2] = before_ref[...]
        wide[2 : 2 + blocks] = own_ref[...]
        wide[2 + blocks : 4 + blocks] = after_ref[...]
        total[...] = jnp.zeros_like(total)

    for k in range(per_step):
        at = index * per_step + k
        coef = coef_ref[k]

        def times(weight, source):
            return jnp.dot(weight, source, preferred_element_type=jnp.float32)

        drive = coef[:, 7:8] * times(far_weights_ref[k], far_ref[...])
        for j in range(5):
            drive += coef[:, j : j + 1] * times(weights_ref[k, j], wide[at + j])
        drive += coef[:, 5:6] * times(weights_ref[k, 5], above_ref[at])
        drive += coef[:, 6:7] * times(weights_ref[k, 6], below_ref[at])
        now = tangents_ref[k].astype(jnp.float32)
        advanced_ref[k] = (now + TIME_STEP * (drive - coef[:, 8:9] * now)).astype(jnp.bfloat16)
    rows = advanced_ref[...].reshape(per_step * size, advanced_ref.shape[-1])
    total[...] += lax.dot_general(
        rows, rows, (((0,), (0,)), ((), ())), preferred_element_type=jnp.float32
    )

    @pl.when(index == pl.num_programs(0) - 1)
    def _():
        gram_ref[...] = jnp.zeros_like(gram_ref)
        for i, j, at in packed_places(total.shape[0], gram_ref.shape[0] // 2):
            gram_ref[at : at + LANES] = total[
                i * LANES : (i + 1) * LANES, j * LANES : (j + 1) * LANES
            ]


def advance(tangents, before, own, after, above, below, far, weights, far_weights, coef):
    blocks, size, vectors = tangents.shape
    half = half_rows(vectors, lax.axis_size("col") * lax.axis_size("layer") // 2)
    per_step = 2 if blocks % 2 == 0 else 1
    whole = pl.BlockSpec(memory_space=pltpu.VMEM)

    def split(*rest):
        return pl.BlockSpec((per_step,) + rest, lambda i: (i,) + (0,) * len(rest))

    return pl.pallas_call(
        functools.partial(advance_kernel, per_step),
        grid=(blocks // per_step,),
        out_shape=(
            jax.ShapeDtypeStruct(tangents.shape, jnp.bfloat16),
            jax.ShapeDtypeStruct((2 * half, LANES), jnp.float32),
        ),
        in_specs=[
            split(size, vectors),
            whole, whole, whole, whole, whole, whole,
            split(7, size, size),
            split(size, far.shape[0]),
            split(size, coef.shape[-1]),
        ],
        out_specs=(split(size, vectors), pl.BlockSpec((2 * half, LANES), lambda i: (0, 0))),
        scratch_shapes=[
            pltpu.VMEM((blocks + 4, size, vectors), jnp.bfloat16),
            pltpu.VMEM((vectors, vectors), jnp.float32),
        ],
        compiler_params=pltpu.CompilerParams(
            vmem_limit_bytes=48 * 1024 * 1024, dimension_semantics=("arbitrary",)
        ),
        name="advance",
    )(tangents, before, own, after, above, below, far, weights, far_weights, coef)


def place_kernel(target_ref, got_ref, out_ref):
    sources, capacity, size, _ = got_ref.shape
    out_ref[...] = jnp.zeros_like(out_ref)
    for s in range(sources):

        def add(c, carry):
            at = target_ref[s, c]
            lanes = slice(s * size, (s + 1) * size)
            held = out_ref[at, :, lanes].astype(jnp.float32)
            out_ref[at, :, lanes] = (held + got_ref[s, c].astype(jnp.float32)).astype(jnp.bfloat16)
            return carry

        lax.fori_loop(0, capacity, add, 0)


def placed(got_weights, got_target, blocks):
    sources, _, size, _ = got_weights.shape
    return pl.pallas_call(
        place_kernel,
        out_shape=jax.ShapeDtypeStruct((blocks, size, sources * size), jnp.bfloat16),
        in_specs=[
            pl.BlockSpec(memory_space=pltpu.SMEM),
            pl.BlockSpec(memory_space=pltpu.VMEM),
        ],
        out_specs=pl.BlockSpec(memory_space=pltpu.VMEM),
        compiler_params=pltpu.CompilerParams(vmem_limit_bytes=32 * 1024 * 1024),
        name="place_pairs",
    )(got_target, got_weights)


def body(
    tangents,
    voltage,
    conductance,
    local_weights,
    block_label,
    pair_dest,
    pair_target,
    bundle_source,
    pair_weights,
):
    lay_blocks, col_blocks, size, vectors = tangents.shape
    steps = voltage.shape[0]
    blocks = col_blocks
    col_count = lax.axis_size("col")
    lay_count = lax.axis_size("layer")
    destination = pair_dest[0, 0, :, 0]
    target_block = pair_target[0, 0]
    bundle_row = bundle_source[0, 0]
    pair_count = destination.shape[0]
    capacity = max(2, 2 * pair_count // col_count)
    slot_count = col_count * capacity
    neurons = float(blocks * size * col_count * lay_count)
    layer = lax.axis_index("layer")
    col_start = lax.axis_index("col") * blocks

    pair_order = jnp.arange(pair_count, dtype=jnp.int32)
    earlier = (destination[:, None] == destination[None, :]) & (
        pair_order[None, :] < pair_order[:, None]
    )
    slot_index = destination * capacity + jnp.sum(earlier.astype(jnp.int32), axis=1)
    placement = jnp.arange(slot_count, dtype=jnp.int32)[:, None] == slot_index[None, :]
    slot_target = jnp.sum(jnp.where(placement, target_block[None, :], 0), axis=1)
    slot_weights = jnp.dot(
        placement.astype(jnp.bfloat16),
        pair_weights[0, 0].reshape(pair_count, size * size),
        preferred_element_type=jnp.float32,
    ).astype(jnp.bfloat16)
    bundle_pick = (
        bundle_row[:, None] == jnp.arange(blocks, dtype=jnp.int32)[None, :]
    )

    def bundle(cells):
        picked = jnp.dot(
            bundle_pick.astype(jnp.bfloat16), cells.reshape(blocks, -1),
            preferred_element_type=jnp.float32,
        )
        return picked.astype(jnp.bfloat16).reshape(col_count, size, vectors)

    volt = voltage[:, 0]
    slope = gain_slope(volt)
    state = tangents[0]
    scaled = (state * slope[0][..., None]).astype(jnp.bfloat16)
    edges = neighbours(scaled)
    far = exchanged(bundle(scaled))
    got_weights = exchanged(slot_weights.reshape(col_count, capacity, size, size))
    bundle_slope = jnp.sum(
        jnp.where(bundle_pick[:, :, None, None], slope.transpose(1, 0, 2)[None], 0.0), axis=1
    )
    target_row = jnp.pad(
        slot_target.astype(jnp.float32).reshape(col_count, 1, capacity),
        ((0, 0), (0, 0), (0, size - capacity)),
    )
    far_notes = exchanged(jnp.concatenate([bundle_slope, target_row], axis=1))
    far_slope = far_notes[:, :steps]
    got_target = far_notes[:, steps, :capacity].astype(jnp.int32)
    edge_slope = [
        edge.transpose(1, 0, 2) for edge in neighbours(slope.transpose(1, 0, 2))
    ]
    far_weights = placed(got_weights, got_target, blocks)

    reversal = jnp.where(block_label == 1, INHIBIT_REVERSAL, EXCITE_REVERSAL).astype(jnp.float32)
    edge_row = jnp.full((1, reversal.shape[1]), EXCITE_REVERSAL, jnp.float32)
    reversal = jnp.concatenate([edge_row, reversal, edge_row], axis=0)
    reversal = jnp.concatenate([reversal[:, -2:], reversal, reversal[:, :2]], axis=1)
    near = lax.dynamic_slice(reversal, (layer, col_start), (3, blocks + 4))
    potential = jnp.stack(
        [near[1, j : j + blocks] for j in range(5)]
        + [near[0, 2 : 2 + blocks], near[2, 2 : 2 + blocks], jnp.full((blocks,), EXCITE_REVERSAL)],
        axis=-1,
    )

    growth = jnp.zeros((vectors,), jnp.float32)
    for t in range(steps):
        coef = jnp.concatenate(
            [
                potential[:, None, :] - volt[t][..., None],
                conductance[t, 0][..., None],
                jnp.zeros((blocks, size, 7), jnp.float32),
            ],
            axis=-1,
        )
        advanced, gram = advance(
            state, edges[0], scaled, edges[1], edges[2], edges[3],
            far.reshape(col_count * size, vectors), local_weights[0], far_weights, coef,
        )
        gram = summed(gram)
        last = t == steps - 1
        if not last:
            gram, advanced = lax.optimization_barrier((gram, advanced))
            edges = neighbours(advanced)
            far = exchanged(bundle(advanced))
        upper, grown = orthonormalize(gram, neurons, vectors)
        growth = growth + grown

        def rotated(cells):
            return jnp.dot(cells, upper, preferred_element_type=jnp.float32).astype(jnp.bfloat16)

        state = rotated(advanced)
        if not last:
            scaled = (state * slope[t + 1][..., None]).astype(jnp.bfloat16)
            edges = [
                (rotated(edge) * edge_slope[k][t + 1][..., None]).astype(jnp.bfloat16)
                for k, edge in enumerate(edges)
            ]
            far = (rotated(far) * far_slope[:, t + 1, :, None]).astype(jnp.bfloat16)
    return state[None], growth


def solution(mesh):
    in_specs = (
        P("layer", "col", None, None),
        P(None, "layer", "col", None),
        P(None, "layer", "col", None),
        P("layer", "col", None, None, None),
        P(),
        P("layer", "col", None, None),
        P("layer", "col", None),
        P("layer", "col", None),
        P("layer", "col", None, None, None),
    )
    out_specs = (P("layer", "col", None, None), P())
    return jax.shard_map(body, mesh=mesh, in_specs=in_specs, out_specs=out_specs, check_vma=False)
```

```python
import functools

import jax
import jax.numpy as jnp
from jax import lax
from jax.experimental import pallas as pl
from jax.experimental.pallas import tpu as pltpu
from jax.sharding import PartitionSpec as P

EXCITE_REVERSAL = 1.0
INHIBIT_REVERSAL = -0.5
THRESHOLD = 0.2
SIGMOID_WIDTH = 0.1
TIME_STEP = 0.1
HI = lax.Precision.HIGHEST
NB = 128
ROWS = 8
MESH = pl.DeviceIdType.MESH
LANES = 128


def half_rows(vectors, chunks):
    count = -(-vectors // LANES)
    rows = -(-(count * (count + 1) // 2) // 2) * LANES
    return -(-rows // (8 * chunks)) * 8 * chunks


def packed_places(vectors, half):
    count = -(-vectors // LANES)
    pairs = [(i, j) for i in range(count) for j in range(i + 1)]
    each = -(-len(pairs) // 2)
    return [(i, j, (k // each) * half + (k % each) * LANES) for k, (i, j) in enumerate(pairs)]


def sum_kernel(groups, per_col, packed_ref, total_ref, mate_in, part, arrived, sems):
    chunk = part.shape[1]
    half = groups * chunk
    col, layer = lax.axis_index("col"), lax.axis_index("layer")
    core = lax.rem(layer, 2)
    mate = {"col": col, "layer": layer + 1 - 2 * core}
    me = col * per_col + layer // 2

    def peer(step):
        k = lax.rem(me + step, groups)
        return k, {"col": k // per_col, "layer": lax.rem(k, per_col) * 2 + core}

    def remote(source, target, kind, sent, got, device):
        return pltpu.make_async_remote_copy(
            src_ref=source,
            dst_ref=target,
            send_sem=sems.at[kind, sent],
            recv_sem=sems.at[kind + 1, got],
            device_id=device,
            device_id_type=MESH,
        )

    barrier = pltpu.get_barrier_semaphore()
    pl.semaphore_signal(barrier, inc=1, device_id=mate, device_id_type=MESH)

    def greet(step, carry):
        _, device = peer(step)
        pl.semaphore_signal(barrier, inc=1, device_id=device, device_id_type=MESH)
        return carry

    lax.fori_loop(1, groups, greet, 0)
    pl.semaphore_wait(barrier, groups)

    mine = pl.multiple_of(core * half, 8)
    other = pl.multiple_of((1 - core) * half, 8)
    swap = remote(packed_ref.at[pl.ds(other, half)], mate_in, 6, 0, 0, mate)
    swap.start()
    swap.wait()
    part[...] = (packed_ref[pl.ds(mine, half), :] + mate_in[...]).reshape(part.shape)

    def scatter(step, carry):
        k, device = peer(step)
        remote(part.at[k], arrived.at[me], 0, k, me, device).start()
        return carry

    def scattered(step, carry):
        k, device = peer(step)
        copy = remote(part.at[k], arrived.at[k], 0, k, k, device)
        copy.wait_send()
        copy.wait_recv()
        return carry

    lax.fori_loop(1, groups, scatter, 0)
    arrived[me] = part[me]
    lax.fori_loop(1, groups, scattered, 0)

    def place(k):
        return total_ref.at[pl.ds(pl.multiple_of(core * half + k * chunk, 8), chunk)]

    def mate_place(k):
        return total_ref.at[pl.ds(pl.multiple_of((1 - core) * half + k * chunk, 8), chunk)]

    place(me)[...] = jnp.sum(arrived[...], axis=0)

    def spread(step, carry):
        k, device = peer(step)
        remote(place(me), place(me), 2, k, me, device).start()
        return carry

    def forward(step, carry):
        k, device = peer(step)
        copy = remote(place(me), place(k), 2, k, k, device)
        copy.wait_recv()
        remote(place(k), place(k), 4, k, k, mate).start()
        return carry

    def finish(step, carry):
        k, device = peer(step)
        remote(place(me), place(k), 2, k, k, device).wait_send()
        copy = remote(place(k), mate_place(k), 4, k, k, mate)
        copy.wait_send()
        copy.wait_recv()
        return carry

    lax.fori_loop(1, groups, spread, 0)
    own = remote(place(me), place(me), 4, me, me, mate)
    own.start()
    lax.fori_loop(1, groups, forward, 0)
    last = remote(place(me), mate_place(me), 4, me, me, mate)
    last.wait_send()
    last.wait_recv()
    lax.fori_loop(1, groups, finish, 0)


def summed(packed):
    per_col = lax.axis_size("layer") // 2
    groups = lax.axis_size("col") * per_col
    half = packed.shape[0] // 2
    chunk = half // groups
    return pl.pallas_call(
        functools.partial(sum_kernel, groups, per_col),
        out_shape=jax.ShapeDtypeStruct(packed.shape, packed.dtype),
        in_specs=[pl.BlockSpec(memory_space=pltpu.VMEM)],
        out_specs=pl.BlockSpec(memory_space=pltpu.VMEM),
        scratch_shapes=[
            pltpu.VMEM((half, LANES), packed.dtype),
            pltpu.VMEM((groups, chunk, LANES), packed.dtype),
            pltpu.VMEM((groups, chunk, LANES), packed.dtype),
            pltpu.SemaphoreType.DMA((8, groups)),
        ],
        compiler_params=pltpu.CompilerParams(
            collective_id=0, has_side_effects=True, vmem_limit_bytes=16 * 1024 * 1024
        ),
        cost_estimate=pl.CostEstimate(flops=0, bytes_accessed=80_000_000, transcendentals=0),
        name="sum_gram",
    )(packed)


def inverse_factor(block):
    n = block.shape[0]
    lane = lax.broadcasted_iota(jnp.int32, (ROWS, n), 1)
    sub = lax.broadcasted_iota(jnp.int32, (ROWS, n), 0)
    tiles = [block[t * ROWS : (t + 1) * ROWS] for t in range(n // ROWS)]
    for first in range(n // ROWS):
        start = first * ROWS
        inside = (lane >= start) & (lane < start + ROWS)
        head = tiles[first]
        cols = [jnp.broadcast_to(head[:, start + q : start + q + 1], (ROWS, n)) for q in range(ROWS)]
        head = jnp.where(lane == sub + start, 1.0, jnp.where(inside, 0.0, head))
        pivots, crossed, kept = [], [], []
        scale = jnp.zeros((ROWS, n), jnp.float32)
        for q in range(ROWS):
            pivot = cols[q][q : q + 1]
            inv = 1.0 / pivot
            factor = jnp.where(sub > q, cols[q] * inv, 0.0)
            ahead = {r: cols[r][q : q + 1] for r in range(q + 1, ROWS)}
            for r in range(q + 1, ROWS):
                cols[r] = cols[r] - factor * ahead[r]
            row = head[q : q + 1]
            head = head - factor * row
            scale = jnp.where(sub == q, lax.rsqrt(pivot), scale)
            pivots.append(inv)
            crossed.append(ahead)
            kept.append(row)
        tiles[first] = head * scale
        for t in range(first + 1, n // ROWS):
            tile = tiles[t]
            cols_t = [jnp.broadcast_to(tile[:, start + q : start + q + 1], (ROWS, n)) for q in range(ROWS)]
            tile = jnp.where(inside, 0.0, tile)
            for q in range(ROWS):
                factor = cols_t[q] * pivots[q]
                for r in range(q + 1, ROWS):
                    cols_t[r] = cols_t[r] - factor * crossed[q][r]
                tile = tile - factor * kept[q]
            tiles[t] = tile
    out = jnp.concatenate(tiles, axis=0)
    rows_id = lax.broadcasted_iota(jnp.int32, (n, n), 0)
    cols_id = lax.broadcasted_iota(jnp.int32, (n, n), 1)
    return jnp.where(rows_id >= cols_id, out, 0.0)


def orthonormal_kernel(count, packed_ref, upper_ref, growth_ref, work):
    n = upper_ref.shape[0]
    for i, j, at in packed_places(n, packed_ref.shape[0] // 2):
        block = packed_ref[at : at + LANES] * (1.0 / count)
        work[i * LANES : (i + 1) * LANES, j * LANES : (j + 1) * LANES] = block
        if i > j:
            work[j * LANES : (j + 1) * LANES, i * LANES : (i + 1) * LANES] = block.T
    cols_id = lax.broadcasted_iota(jnp.int32, (NB, n), 1)

    def step(i, carry):
        at = pl.multiple_of(i * NB, NB)
        diag = inverse_factor(work[pl.ds(at, NB), pl.ds(at, NB)])
        work[:, pl.ds(at, NB)] = jnp.zeros((n, NB), jnp.float32)
        rows = jnp.dot(diag, work[pl.ds(at, NB), :], precision=HI, preferred_element_type=jnp.float32)
        work[pl.ds(at, NB), :] = rows
        work[pl.ds(at, NB), pl.ds(at, NB)] = diag
        rows = work[pl.ds(at, NB), :]
        panel = jnp.where(cols_id >= at + NB, rows, 0.0)
        work[...] -= lax.dot_general(
            panel, rows, (((0,), (0,)), ((), ())), precision=HI, preferred_element_type=jnp.float32
        )
        return carry

    lax.fori_loop(0, n // NB, step, 0)
    rows_n = lax.broadcasted_iota(jnp.int32, (n, n), 0)
    cols_n = lax.broadcasted_iota(jnp.int32, (n, n), 1)
    full = work[...]
    upper_ref[...] = jnp.where(rows_n >= cols_n, full, 0.0).T.astype(jnp.bfloat16)
    growth_ref[...] = -jnp.log(jnp.sum(jnp.where(rows_n == cols_n, full, 0.0), axis=0, keepdims=True))


def orthonormalize(gram_total, count, n):
    upper, growth = pl.pallas_call(
        functools.partial(orthonormal_kernel, count),
        out_shape=(
            jax.ShapeDtypeStruct((n, n), jnp.bfloat16),
            jax.ShapeDtypeStruct((1, n), jnp.float32),
        ),
        in_specs=[pl.BlockSpec(memory_space=pltpu.VMEM)],
        out_specs=(pl.BlockSpec(memory_space=pltpu.VMEM), pl.BlockSpec(memory_space=pltpu.VMEM)),
        scratch_shapes=[pltpu.VMEM((n, n), jnp.float32)],
        compiler_params=pltpu.CompilerParams(vmem_limit_bytes=16 * 1024 * 1024),
        cost_estimate=pl.CostEstimate(flops=30_000_000_000, bytes_accessed=90_000_000, transcendentals=n),
        name="orthonormalize",
    )(gram_total)
    return upper, growth[0]


def gain_slope(volt_now):
    sigma_value = jax.nn.sigmoid((volt_now - THRESHOLD) / SIGMOID_WIDTH)
    return sigma_value * (1.0 - sigma_value) / SIGMOID_WIDTH


def shifted(value, axis, step, closed):
    count = lax.axis_size(axis)
    pairs = [(i, i + step) for i in range(count)]
    if closed:
        pairs = [(i, j % count) for i, j in pairs]
    else:
        pairs = [(i, j) for i, j in pairs if 0 <= j < count]
    return lax.ppermute(value, axis, pairs)


def column_edges(cells):
    return shifted(cells[-2:], "col", 1, True), shifted(cells[:2], "col", -1, True)


def layer_edges(cells):
    return shifted(cells, "layer", 1, False), shifted(cells, "layer", -1, False)


def exchanged(value):
    return lax.all_to_all(value, "col", split_axis=0, concat_axis=0, tiled=True)


def advance_kernel(
    per_step, tangents_ref, before_ref, own_ref, after_ref, above_ref, below_ref, far_ref,
    weights_ref, far_weights_ref, coef_ref, advanced_ref, gram_ref, wide, total
):
    index = pl.program_id(0)
    blocks, size, _ = own_ref.shape

    @pl.when(index == 0)
    def _():
        wide[0:2] = before_ref[...]
        wide[2 : 2 + blocks] = own_ref[...]
        wide[2 + blocks : 4 + blocks] = after_ref[...]
        total[...] = jnp.zeros_like(total)

    for k in range(per_step):
        at = index * per_step + k
        coef = coef_ref[k]

        def times(weight, source):
            return jnp.dot(weight, source, preferred_element_type=jnp.float32)

        drive = coef[:, 7:8] * times(far_weights_ref[k], far_ref[...])
        for j in range(5):
            drive += coef[:, j : j + 1] * times(weights_ref[k, j], wide[at + j])
        drive += coef[:, 5:6] * times(weights_ref[k, 5], above_ref[at])
        drive += coef[:, 6:7] * times(weights_ref[k, 6], below_ref[at])
        now = tangents_ref[k].astype(jnp.float32)
        advanced_ref[k] = (now + TIME_STEP * (drive - coef[:, 8:9] * now)).astype(jnp.bfloat16)
    rows = advanced_ref[...].reshape(per_step * size, advanced_ref.shape[-1])
    total[...] += lax.dot_general(
        rows, rows, (((0,), (0,)), ((), ())), preferred_element_type=jnp.float32
    )

    @pl.when(index == pl.num_programs(0) - 1)
    def _():
        gram_ref[...] = jnp.zeros_like(gram_ref)
        for i, j, at in packed_places(total.shape[0], gram_ref.shape[0] // 2):
            gram_ref[at : at + LANES] = total[
                i * LANES : (i + 1) * LANES, j * LANES : (j + 1) * LANES
            ]


def advance(tangents, before, own, after, above, below, far, weights, far_weights, coef):
    blocks, size, vectors = tangents.shape
    half = half_rows(vectors, lax.axis_size("col") * lax.axis_size("layer") // 2)
    per_step = 2 if blocks % 2 == 0 else 1
    whole = pl.BlockSpec(memory_space=pltpu.VMEM)

    def split(*rest):
        return pl.BlockSpec((per_step,) + rest, lambda i: (i,) + (0,) * len(rest))

    return pl.pallas_call(
        functools.partial(advance_kernel, per_step),
        grid=(blocks // per_step,),
        out_shape=(
            jax.ShapeDtypeStruct(tangents.shape, jnp.bfloat16),
            jax.ShapeDtypeStruct((2 * half, LANES), jnp.float32),
        ),
        in_specs=[
            split(size, vectors),
            whole, whole, whole, whole, whole, whole,
            split(7, size, size),
            split(size, far.shape[0]),
            split(size, coef.shape[-1]),
        ],
        out_specs=(split(size, vectors), pl.BlockSpec((2 * half, LANES), lambda i: (0, 0))),
        scratch_shapes=[
            pltpu.VMEM((blocks + 4, size, vectors), jnp.bfloat16),
            pltpu.VMEM((vectors, vectors), jnp.float32),
        ],
        compiler_params=pltpu.CompilerParams(
            vmem_limit_bytes=48 * 1024 * 1024, dimension_semantics=("arbitrary",)
        ),
        name="advance",
    )(tangents, before, own, after, above, below, far, weights, far_weights, coef)


def exchange_kernel(parts, *refs):
    given, got, sems = refs[:parts], refs[parts : 2 * parts], refs[2 * parts]
    count = given[0].shape[0]
    me, layer = lax.axis_index("col"), lax.axis_index("layer")
    barrier = pltpu.get_barrier_semaphore()

    def peer(step):
        k = lax.rem(me + step, count)
        return k, {"col": k, "layer": layer}

    def remote(part, k, slot, device):
        return pltpu.make_async_remote_copy(
            src_ref=given[part].at[k],
            dst_ref=got[part].at[slot],
            send_sem=sems.at[2 * part, k],
            recv_sem=sems.at[2 * part + 1, slot],
            device_id=device,
            device_id_type=MESH,
        )

    def greet(step, carry):
        _, device = peer(step)
        pl.semaphore_signal(barrier, inc=1, device_id=device, device_id_type=MESH)
        return carry

    def send(step, carry):
        k, device = peer(step)
        for part in range(parts):
            remote(part, k, me, device).start()
        return carry

    def receive(step, carry):
        k, device = peer(step)
        for part in range(parts):
            copy = remote(part, k, k, device)
            copy.wait_send()
            copy.wait_recv()
        return carry

    lax.fori_loop(1, count, greet, 0)
    pl.semaphore_wait(barrier, count - 1)
    lax.fori_loop(1, count, send, 0)
    for part in range(parts):
        got[part][me] = given[part][me]
    lax.fori_loop(1, count, receive, 0)


def exchanged_together(*values):
    parts = len(values)
    vmem = pl.BlockSpec(memory_space=pltpu.VMEM)
    return pl.pallas_call(
        functools.partial(exchange_kernel, parts),
        out_shape=tuple(jax.ShapeDtypeStruct(v.shape, v.dtype) for v in values),
        in_specs=[vmem] * parts,
        out_specs=(vmem,) * parts,
        scratch_shapes=[pltpu.SemaphoreType.DMA((2 * parts, values[0].shape[0]))],
        compiler_params=pltpu.CompilerParams(
            collective_id=1, has_side_effects=True, vmem_limit_bytes=24 * 1024 * 1024
        ),
        cost_estimate=pl.CostEstimate(
            flops=0, bytes_accessed=200_000_000, transcendentals=0
        ),
        name="exchange",
    )(*values)


def place_kernel(target_ref, got_ref, out_ref):
    sources, capacity, size, _ = got_ref.shape
    out_ref[...] = jnp.zeros_like(out_ref)
    for s in range(sources):

        def add(c, carry):
            at = target_ref[s, c]
            lanes = slice(s * size, (s + 1) * size)
            held = out_ref[at, :, lanes].astype(jnp.float32)
            out_ref[at, :, lanes] = (held + got_ref[s, c].astype(jnp.float32)).astype(jnp.bfloat16)
            return carry

        lax.fori_loop(0, capacity, add, 0)


def placed(got_weights, got_target, blocks):
    sources, _, size, _ = got_weights.shape
    return pl.pallas_call(
        place_kernel,
        out_shape=jax.ShapeDtypeStruct((blocks, size, sources * size), jnp.bfloat16),
        in_specs=[
            pl.BlockSpec(memory_space=pltpu.SMEM),
            pl.BlockSpec(memory_space=pltpu.VMEM),
        ],
        out_specs=pl.BlockSpec(memory_space=pltpu.VMEM),
        compiler_params=pltpu.CompilerParams(vmem_limit_bytes=32 * 1024 * 1024),
        name="place_pairs",
    )(got_target, got_weights)


def body(
    tangents,
    voltage,
    conductance,
    local_weights,
    block_label,
    pair_dest,
    pair_target,
    bundle_source,
    pair_weights,
):
    lay_blocks, col_blocks, size, vectors = tangents.shape
    steps = voltage.shape[0]
    blocks = col_blocks
    col_count = lax.axis_size("col")
    lay_count = lax.axis_size("layer")
    destination = pair_dest[0, 0, :, 0]
    target_block = pair_target[0, 0]
    bundle_row = bundle_source[0, 0]
    pair_count = destination.shape[0]
    capacity = max(2, 2 * pair_count // col_count)
    slot_count = col_count * capacity
    neurons = float(blocks * size * col_count * lay_count)
    layer = lax.axis_index("layer")
    col_start = lax.axis_index("col") * blocks

    pair_order = jnp.arange(pair_count, dtype=jnp.int32)
    earlier = (destination[:, None] == destination[None, :]) & (
        pair_order[None, :] < pair_order[:, None]
    )
    slot_index = destination * capacity + jnp.sum(earlier.astype(jnp.int32), axis=1)
    placement = jnp.arange(slot_count, dtype=jnp.int32)[:, None] == slot_index[None, :]
    slot_target = jnp.sum(jnp.where(placement, target_block[None, :], 0), axis=1)
    slot_weights = jnp.dot(
        placement.astype(jnp.bfloat16),
        pair_weights[0, 0].reshape(pair_count, size * size),
        preferred_element_type=jnp.float32,
    ).astype(jnp.bfloat16)
    bundle_pick = (
        bundle_row[:, None] == jnp.arange(blocks, dtype=jnp.int32)[None, :]
    )

    def bundle(cells):
        picked = jnp.dot(
            bundle_pick.astype(jnp.bfloat16), cells.reshape(blocks, -1),
            preferred_element_type=jnp.float32,
        )
        return picked.astype(jnp.bfloat16).reshape(col_count, size, vectors)

    volt = voltage[:, 0]
    slope = gain_slope(volt)
    state = tangents[0]
    scaled = (state * slope[0][..., None]).astype(jnp.bfloat16)
    slope_rows = slope.transpose(1, 0, 2)
    edge_slope = [
        edge.transpose(1, 0, 2) for edge in column_edges(slope_rows) + layer_edges(slope_rows)
    ]
    beside = column_edges(scaled)
    over = layer_edges(scaled)
    bundle_slope = jnp.sum(
        jnp.where(bundle_pick[:, :, None, None], slope.transpose(1, 0, 2)[None], 0.0), axis=1
    )
    target_row = jnp.pad(
        slot_target.astype(jnp.float32).reshape(col_count, 1, capacity),
        ((0, 0), (0, 0), (0, size - capacity)),
    )
    notes = jnp.concatenate([bundle_slope, target_row], axis=1)
    notes = jnp.pad(notes, ((0, 0), (0, -notes.shape[1] % 8), (0, 0)))
    sent = (slot_weights.reshape(col_count, capacity, size, size), bundle(scaled), notes)
    sent, beside = lax.optimization_barrier((sent, beside))
    got_weights, far, far_notes = exchanged_together(*sent)
    far_slope = far_notes[:, :steps]
    got_target = far_notes[:, steps, :capacity].astype(jnp.int32)
    far_weights = placed(got_weights, got_target, blocks)

    reversal = jnp.where(block_label == 1, INHIBIT_REVERSAL, EXCITE_REVERSAL).astype(jnp.float32)
    edge_row = jnp.full((1, reversal.shape[1]), EXCITE_REVERSAL, jnp.float32)
    reversal = jnp.concatenate([edge_row, reversal, edge_row], axis=0)
    reversal = jnp.concatenate([reversal[:, -2:], reversal, reversal[:, :2]], axis=1)
    near = lax.dynamic_slice(reversal, (layer, col_start), (3, blocks + 4))
    potential = jnp.stack(
        [near[1, j : j + blocks] for j in range(5)]
        + [near[0, 2 : 2 + blocks], near[2, 2 : 2 + blocks], jnp.full((blocks,), EXCITE_REVERSAL)],
        axis=-1,
    )

    growth = jnp.zeros((vectors,), jnp.float32)
    for t in range(steps):
        coef = jnp.concatenate(
            [
                potential[:, None, :] - volt[t][..., None],
                conductance[t, 0][..., None],
                jnp.zeros((blocks, size, 7), jnp.float32),
            ],
            axis=-1,
        )
        advanced, gram = advance(
            state, beside[0], scaled, beside[1], over[0], over[1],
            far.reshape(col_count * size, vectors), local_weights[0], far_weights, coef,
        )
        last = t == steps - 1
        if not last:
            beside = column_edges(advanced)
        gram = summed(gram)
        if not last:
            gram, advanced, beside, edge_slope = lax.optimization_barrier(
                (gram, advanced, beside, edge_slope)
            )
            over = layer_edges(advanced)
            far = exchanged(bundle(advanced))
        upper, grown = orthonormalize(gram, neurons, vectors)
        growth = growth + grown

        def rotated(cells):
            return jnp.dot(cells, upper, preferred_element_type=jnp.float32).astype(jnp.bfloat16)

        state = rotated(advanced)
        if not last:
            scaled = (state * slope[t + 1][..., None]).astype(jnp.bfloat16)
            edges = [
                (rotated(edge) * edge_slope[k][t + 1][..., None]).astype(jnp.bfloat16)
                for k, edge in enumerate(beside + over)
            ]
            beside, over = edges[:2], edges[2:]
            far = (rotated(far) * far_slope[:, t + 1, :, None]).astype(jnp.bfloat16)
    return state[None], growth


def solution(mesh):
    in_specs = (
        P("layer", "col", None, None),
        P(None, "layer", "col", None),
        P(None, "layer", "col", None),
        P("layer", "col", None, None, None),
        P(),
        P("layer", "col", None, None),
        P("layer", "col", None),
        P("layer", "col", None),
        P("layer", "col", None, None, None),
    )
    out_specs = (P("layer", "col", None, None), P())
    return jax.shard_map(body, mesh=mesh, in_specs=in_specs, out_specs=out_specs, check_vma=False)
```
